512 devices in a mesh: orb: 64 (over z, y), st: 8 (over x, core).
Axes of the slice: x: 4, y: 4, z: 16, core: 2. Of those that a mesh axis runs over, the one named last changes fastest.
Arguments:
- wavefunction: float32 [2, 1024, 65536], P(None, 'st', 'orb'), may hold values from -6 to 6
- slope_prev: float32 [2, 1024, 65536], P(None, 'st', 'orb'), may hold values from -6 to 6
- hopping: bfloat16 [1024, 14, 64, 64], P('orb', None, 'st'), may hold values from -0.1875 to 0.1875
- offsets: int32 [1024, 14], P('orb'), may hold values from -16 to 16
- counts: int32 [1024], P('orb'), may hold values from 7 to 14
- bond_vectors: float32 [3, 1024, 14], P(None, 'orb'), may hold values from -6 to 6
- shifts: int32 [3, 1024, 14], P(None, 'orb'), may hold values from -1 to 1
- vector_potential: float32 [3], replicated, may hold values from -1 to 1
Outputs:
- slope_next: float32 [2, 1024, 65536], P(None, 'st', 'orb')
The draws below stay inside these ranges and needn't reach their ends.
All inputs are finite; a program needn't handle non-finite values.
Results may differ from the reference program's by a relative error of at most 0.0003.
Values may be sent and summed in bfloat16 or wider, within the bound.
No kernel may reach another device: no remote copies, remote signals or barrier semaphores. Data moves between devices by JAX's collectives and lax.ppermute only.
A program may use at most 64 MiB of HBM per device.

```python
import jax
import jax.numpy as jnp
from jax import lax

OB = 64
NNZ = 14
BLK_DEV = 16
BLOCKS = 1024
ORBS = 65536
STATES = 1024


def set_ends(array, stream_key, low, top_value):
    dims = array.shape
    spot = [jax.random.randint(jax.random.fold_in(stream_key, axis), (), 0, dims[axis]) for axis in range(len(dims))]
    array = array.at[tuple(spot)].set(low)
    longest = dims.index(max(dims))
    spot[longest] = (spot[longest] + 1) % dims[longest]
    return array.at[tuple(spot)].set(top_value)


def block_levels(own_key, dims, split, least, high):
    def one(axis_at, shards_of):
        steps = jax.random.uniform(jax.random.fold_in(jax.random.fold_in(own_key, 6), axis_at), (shards_of,), jnp.float32, least / len(split), high / len(split))
        return jnp.repeat(jnp.exp(steps), dims[axis_at] // shards_of).reshape((-1,) + (1,) * (len(dims) - axis_at - 1))

    gain = one(*split[0])
    for cut in split[1:]:
        gain = gain * one(*cut)
    return gain


def bell_draw(rng, dims, spread, bound, cuts=(), held_as=jnp.bfloat16):
    values = jax.random.normal(rng, dims, jnp.float32) * spread
    if len(cuts) > 0:
        values = block_levels(rng, dims, cuts, -0.22, 0.18) * values
    return jnp.clip(values, min=-bound, max=bound).astype(held_as)


def setup_inputs(seed: int = 0) -> dict:
    key_of = jax.random.split(jax.random.key(seed), 9)
    return {
        "wavefunction": bell_draw(key_of[0], (2, STATES, ORBS), 1.0, 6.0, ((1, 8), (2, 64)), jnp.float32),
        "slope_prev": bell_draw(key_of[1], (2, STATES, ORBS), 1.0, 6.0, ((1, 8), (2, 64)), jnp.float32),
        "hopping": bell_draw(key_of[2], (BLOCKS, NNZ, OB, OB), (NNZ * OB) ** -0.5, 0.1875, ((0, 64), (2, 8))),
        "offsets": set_ends(jax.random.randint(key_of[3], (BLOCKS, NNZ), 0 - BLK_DEV, BLK_DEV + 1), jax.random.fold_in(key_of[3], 1), 0 - BLK_DEV, BLK_DEV).astype(jnp.int32),
        "counts": set_ends(jax.random.randint(key_of[4], (BLOCKS,), NNZ // 2, NNZ + 1), jax.random.fold_in(key_of[4], 1), NNZ // 2, NNZ).astype(jnp.int32),
        "bond_vectors": bell_draw(key_of[5], (3, BLOCKS, NNZ), 1.0, 6.0, ((1, 64),), jnp.float32),
        "shifts": set_ends(jax.random.randint(key_of[6], (3, BLOCKS, NNZ), -1, 2), jax.random.fold_in(key_of[6], 1), -1, 1).astype(jnp.int32),
        "vector_potential": jnp.clip(jax.random.uniform(key_of[7], (3,), jnp.float32, -1.0, 1.0), -1.0, 1.0),
    }


def reference(wavefunction, slope_prev, hopping, offsets, counts, bond_vectors, shifts, vector_potential):
    segment = (wavefunction + 0.25 * slope_prev).reshape(2, STATES, BLOCKS, OB)
    theta = jnp.zeros((BLOCKS, NNZ), jnp.float32)
    for axis_index in range(3):
        theta = theta + vector_potential[axis_index] * (bond_vectors[axis_index] + 2.0 * shifts[axis_index].astype(jnp.float32))
    live = (jnp.arange(NNZ, dtype=jnp.int32)[None, :] < counts[:, None]).astype(jnp.float32)
    cosine = jnp.cos(theta) * live
    sine = jnp.sin(theta) * live
    row_index = jnp.arange(BLOCKS, dtype=jnp.int32)
    total_re = jnp.zeros((STATES, BLOCKS, OB), jnp.float32)
    total_im = jnp.zeros((STATES, BLOCKS, OB), jnp.float32)
    for slot_index in range(NNZ):
        columns = ((row_index + offsets[:, slot_index]) % BLOCKS).astype(jnp.int32)
        picked = jnp.take(segment, columns, axis=2)
        tile_slab = hopping[:, slot_index].astype(jnp.float32)
        product = jnp.einsum('iab,nsib->nsia', tile_slab, picked, precision=lax.Precision.HIGHEST)
        cos_w = cosine[None, :, slot_index, None]
        sin_w = sine[None, :, slot_index, None]
        total_re = total_re + cos_w * product[1] + sin_w * product[0]
        total_im = total_im + sin_w * product[1] - cos_w * product[0]
    return jnp.stack([total_re, total_im]).reshape(2, STATES, ORBS)
```

```python
import functools

import jax
import jax.numpy as jnp
from jax import lax
from jax.experimental import pallas as pl
from jax.experimental.pallas import tpu as pltpu
from jax.sharding import PartitionSpec as P

VMEM = pltpu.VMEM
SMEM = pltpu.SMEM
F32 = jnp.float32
BF16 = jnp.bfloat16
LEVELS = 32767.0
STEPS = 256.0
TINY = 1e-37


def split(x):
    hi = x.astype(BF16)
    return hi, (x - hi.astype(F32)).astype(BF16)


def tiles_kernel(hop_ref, off_ref, cnt_ref, bond_ref, shift_ref, vp_ref, hop_out, cos_out, sin_out, col_out):
    blocks, slots, rows, width = hop_ref.shape
    for i in range(blocks):
        hop_out[i] = jnp.concatenate([hop_ref[i, s] for s in range(slots)], axis=1)
    theta = jnp.zeros(off_ref.shape, F32)
    for k in range(3):
        theta = theta + vp_ref[k] * (bond_ref[k] + 2.0 * shift_ref[k].astype(F32))
    live = lax.broadcasted_iota(jnp.int32, theta.shape, 1) < cnt_ref[...]
    cos_out[...] = jnp.where(live, jnp.cos(theta), 0.0)
    sin_out[...] = jnp.where(live, jnp.sin(theta), 0.0)
    row = lax.broadcasted_iota(jnp.int32, theta.shape, 0)
    col_out[...] = off_ref[...] + row + blocks


def segment_kernel(width, wave_ref, slope_ref, own_ref, pay_ref):
    states = wave_ref.shape[1]
    blocks = wave_ref.shape[2] // width
    codes = []
    for c in range(blocks * width // 128):
        cols = pl.ds(c * 128, 128)
        seg = wave_ref[:, :, cols] + 0.25 * slope_ref[:, :, cols]
        both = jnp.concatenate([seg[0].T, seg[1].T], axis=1)
        hi, lo = split(both)
        for k in range(128 // width):
            j = c * (128 // width) + k
            part = both[k * width : (k + 1) * width]
            own_ref[j, 0:width] = hi[k * width : (k + 1) * width]
            own_ref[j, width : 2 * width] = lo[k * width : (k + 1) * width]
            top = jnp.maximum(jnp.max(jnp.abs(part), axis=0, keepdims=True), TINY)
            code = jnp.ceil(jnp.log2(top) * STEPS) + 1.0
            codes.append(code)
            q = jnp.round(part * (LEVELS * jnp.exp2(code * (-1.0 / STEPS))))
            pay_ref[j * width : (j + 1) * width] = q.astype(jnp.int32).astype(jnp.int16)
    pay_ref[blocks * width :] = jnp.concatenate(codes, axis=0).astype(jnp.int32).astype(jnp.int16)


def slots_kernel(hop_ref, own_ref, prev_ref, next_ref, cos_ref, sin_ref, col_ref, out_ref, xs):
    blocks, rows, depth = hop_ref.shape
    slots = cos_ref.shape[1]
    width = depth // slots
    states = out_ref.shape[1]

    def own(j, _):
        xs[blocks + j] = own_ref[j]
        return 0

    lax.fori_loop(0, blocks, own, 0, unroll=4)
    for base, ref in ((0, prev_ref), (2 * blocks, next_ref)):
        code = ref[blocks * width :].astype(jnp.int32).astype(F32)
        scale = jnp.exp2(code * (1.0 / STEPS)) * (1.0 / LEVELS)
        for j in range(blocks):
            q = ref[j * width : (j + 1) * width].astype(jnp.int32).astype(F32)
            hi, lo = split(q * scale[j : j + 1])
            xs[base + j, 0:width] = hi
            xs[base + j, width : 2 * width] = lo

    def block_pair(pair, _):
        res = []
        for k in range(2):
            i = 2 * pair + k
            a = jnp.zeros((rows, 2 * states), F32)
            b = jnp.zeros((rows, 2 * states), F32)
            for p in range(slots // 2):
                tile = hop_ref[i, :, 2 * width * p : 2 * width * (p + 1)]
                for h in range(2):
                    s = 2 * p + h
                    half = tile[:, h * width : (h + 1) * width]
                    prod = jnp.dot(
                        jnp.concatenate([half, half], axis=1), xs[col_ref[i, s]], preferred_element_type=F32
                    )
                    a = a + cos_ref[i, s] * prod
                    b = b + sin_ref[i, s] * prod
            res.append((a[:, states:] + b[:, :states], b[:, states:] - a[:, :states]))
        cols = pl.ds(pl.multiple_of(pair * 2 * rows, 2 * rows), 2 * rows)
        out_ref[0, :, cols] = jnp.concatenate([res[0][0], res[1][0]], axis=0).T
        out_ref[1, :, cols] = jnp.concatenate([res[0][1], res[1][1]], axis=0).T
        return 0

    lax.fori_loop(0, blocks // 2, block_pair, 0)


def on_device(
    wavefunction, slope_prev, hopping, offsets, counts, bond_vectors, shifts, vector_potential
):
    blocks, slots, rows, width = hopping.shape
    states = wavefunction.shape[1]
    orbs = blocks * width
    table = jax.ShapeDtypeStruct((blocks, slots), F32)
    vm = pl.BlockSpec(memory_space=VMEM)
    sm = pl.BlockSpec(memory_space=SMEM)
    params = pltpu.CompilerParams(vmem_limit_bytes=40 * 1024 * 1024)
    part, cosine, sine, columns = pl.pallas_call(
        tiles_kernel,
        out_shape=(
            jax.ShapeDtypeStruct((blocks, rows, slots * width), BF16),
            table,
            table,
            jax.ShapeDtypeStruct((blocks, slots), jnp.int32),
        ),
        in_specs=[vm] * 5 + [sm],
        out_specs=[vm] * 4,
        compiler_params=params,
        name="tiles",
    )(hopping, offsets, counts[:, None], bond_vectors, shifts, vector_potential)
    tiles = lax.all_gather(part, "st", axis=1, tiled=True)
    own, payload = pl.pallas_call(
        functools.partial(segment_kernel, width),
        out_shape=(
            jax.ShapeDtypeStruct((blocks, 2 * width, 2 * states), BF16),
            jax.ShapeDtypeStruct((orbs + blocks, 2 * states), jnp.int16),
        ),
        in_specs=[vm] * 2,
        out_specs=[vm] * 2,
        compiler_params=params,
        name="segment",
    )(wavefunction, slope_prev)
    size = lax.axis_size("orb")
    up = [(i, (i + 1) % size) for i in range(size)]
    down = [(j, i) for i, j in up]
    before = lax.ppermute(payload, "orb", up)
    after = lax.ppermute(payload, "orb", down)
    return pl.pallas_call(
        slots_kernel,
        out_shape=jax.ShapeDtypeStruct((2, states, orbs), F32),
        in_specs=[vm] * 4 + [sm] * 3,
        out_specs=vm,
        scratch_shapes=[VMEM((3 * blocks, 2 * width, 2 * states), BF16)],
        compiler_params=params,
        name="slots",
    )(tiles, own, before, after, cosine, sine, columns)


def solution(mesh):
    return jax.shard_map(
        on_device,
        mesh=mesh,
        in_specs=(
            P(None, "st", "orb"),
            P(None, "st", "orb"),
            P("orb", None, "st", None),
            P("orb", None),
            P("orb"),
            P(None, "orb", None),
            P(None, "orb", None),
            P(),
        ),
        out_specs=P(None, "st", "orb"),
        check_vma=False,
    )
```

```python
import functools

import jax
import jax.numpy as jnp
from jax import lax
from jax.experimental import pallas as pl
from jax.experimental.pallas import tpu as pltpu
from jax.sharding import PartitionSpec as P

VMEM = pltpu.VMEM
SMEM = pltpu.SMEM
DMA = pltpu.SemaphoreType.DMA
F32 = jnp.float32
BF16 = jnp.bfloat16
I16 = jnp.int16
I32 = jnp.int32
LEVELS = 32767.0
STEPS = 256.0
TINY = 1e-37


def split(x):
    hi = x.astype(BF16)
    return hi, (x - hi.astype(F32)).astype(BF16)


def encode(x):
    size = jnp.abs(x)
    down = jnp.zeros_like(x)
    for k in (64, 32, 16, 8, 4, 2, 1):
        small = size < 2.0**-k
        size = jnp.where(small, size * 2.0**k, size)
        down = jnp.where(small, down + k, down)
    digits = jnp.where(x < 0, -256.0, 256.0) * size
    return ((63.0 - down) * 512.0 + digits + 256.0).astype(I32)


def decode(code):
    power = (code >> 9).astype(F32)
    digits = ((code & 511) - 256).astype(F32)
    return digits * jnp.exp2(power - 71.0)


def prep_kernel(
    width, wave, slope, hop, off, cnt, bond, shift, vp,
    own_ref, pay_ref, hop_out, phase_out,
    wave_v, slope_v, hop_v, bond_v, shift_v, cnt_s, vp_s, sems,
):
    blocks, slots, rows, _ = hop.shape
    pairs = ((hop, hop_v), (bond, bond_v), (shift, shift_v), (cnt, cnt_s), (vp, vp_s), (wave, wave_v), (slope, slope_v))
    copies = [pltpu.make_async_copy(a, b, sems.at[n]) for n, (a, b) in enumerate(pairs)]
    for copy in copies:
        copy.start()
    copies[0].wait()
    for i in range(blocks):
        line = jnp.concatenate([hop_v[i, s].astype(F32) for s in range(slots)], axis=1)
        hop_out[i] = encode(line).astype(I16)
    for copy in copies[1:5]:
        copy.wait()
    theta = jnp.zeros((blocks, slots), F32)
    for k in range(3):
        theta = theta + vp_s[k] * (bond_v[k] + 2.0 * shift_v[k].astype(F32))
    row = lax.broadcasted_iota(I32, (blocks, slots), 0)
    slot = lax.broadcasted_iota(I32, (blocks, slots), 1)
    count = jnp.zeros((blocks, slots), I32)
    for i in range(blocks):
        count = jnp.where(row == i, cnt_s[i], count)
    live = slot < count
    phase_out[0:blocks] = jnp.where(live, jnp.cos(theta), 0.0)
    phase_out[blocks:] = jnp.where(live, jnp.sin(theta), 0.0)
    for copy in copies[5:]:
        copy.wait()
    codes = []
    for c in range(blocks * width // 128):
        cols = pl.ds(c * 128, 128)
        seg = wave_v[:, :, cols] + 0.25 * slope_v[:, :, cols]
        both = jnp.concatenate([seg[0].T, seg[1].T], axis=1)
        hi, lo = split(both)
        for k in range(128 // width):
            j = c * (128 // width) + k
            part = both[k * width : (k + 1) * width]
            own_ref[j, 0:width] = hi[k * width : (k + 1) * width]
            own_ref[j, width : 2 * width] = lo[k * width : (k + 1) * width]
            top = jnp.maximum(jnp.max(jnp.abs(part), axis=0, keepdims=True), TINY)
            code = jnp.ceil(jnp.log2(top) * STEPS) + 1.0
            codes.append(code)
            q = jnp.round(part * (LEVELS * jnp.exp2(code * (-1.0 / STEPS))))
            pay_ref[j * width : (j + 1) * width] = q.astype(I32).astype(I16)
    pay_ref[blocks * width :] = jnp.concatenate(codes, axis=0).astype(I32).astype(I16)


def slots_kernel(hop_ref, own_ref, prev_ref, next_ref, phase, off, out, xs, out_v, phase_s, off_s, sems, out_sems):
    blocks, rows, depth = hop_ref.shape
    slots = off.shape[1]
    width = depth // slots
    states = out.shape[1]
    phase_copy = pltpu.make_async_copy(phase, phase_s, sems.at[0])
    off_copy = pltpu.make_async_copy(off, off_s, sems.at[1])
    phase_copy.start()
    off_copy.start()

    for j in range(blocks):
        xs[blocks + j] = own_ref[j]
    for base, ref in ((0, prev_ref), (2 * blocks, next_ref)):
        code = ref[blocks * width :].astype(I32).astype(F32)
        scale = jnp.exp2(code * (1.0 / STEPS)) * (1.0 / LEVELS)
        for j in range(blocks):
            q = ref[j * width : (j + 1) * width].astype(I32).astype(F32)
            hi, lo = split(q * scale[j : j + 1])
            xs[base + j, 0:width] = hi
            xs[base + j, width : 2 * width] = lo
    phase_copy.wait()
    off_copy.wait()

    def out_copy(pair):
        cols = pl.ds(pl.multiple_of(pair * 2 * rows, 2 * rows), 2 * rows)
        return pltpu.make_async_copy(out_v.at[:, :, cols], out.at[:, :, cols], out_sems.at[pair])

    def block_pair(pair, _):
        res = []
        for k in range(2):
            i = 2 * pair + k
            a = jnp.zeros((rows, 2 * states), F32)
            b = jnp.zeros((rows, 2 * states), F32)
            for p in range(slots // 2):
                tile = decode(hop_ref[i, :, 2 * width * p : 2 * width * (p + 1)].astype(I32)).astype(BF16)
                for h in range(2):
                    s = 2 * p + h
                    half = tile[:, h * width : (h + 1) * width]
                    prod = jnp.dot(
                        jnp.concatenate([half, half], axis=1),
                        xs[off_s[i, s] + (i + blocks)],
                        preferred_element_type=F32,
                    )
                    a = a + phase_s[i, s] * prod
                    b = b + phase_s[blocks + i, s] * prod
            res.append((a[:, states:] + b[:, :states], b[:, states:] - a[:, :states]))
        cols = pl.ds(pl.multiple_of(pair * 2 * rows, 2 * rows), 2 * rows)
        out_v[0, :, cols] = jnp.concatenate([res[0][0], res[1][0]], axis=0).T
        out_v[1, :, cols] = jnp.concatenate([res[0][1], res[1][1]], axis=0).T
        out_copy(pair).start()
        return 0

    lax.fori_loop(0, blocks // 2, block_pair, 0)
    for pair in range(blocks // 2):
        out_copy(pair).wait()


def on_device(
    wavefunction, slope_prev, hopping, offsets, counts, bond_vectors, shifts, vector_potential
):
    blocks, slots, rows, width = hopping.shape
    states = wavefunction.shape[1]
    orbs = blocks * width
    vm = pl.BlockSpec(memory_space=VMEM)
    far = pl.BlockSpec(memory_space=pltpu.HBM)
    own, payload, part, phase = pl.pallas_call(
        functools.partial(prep_kernel, width),
        out_shape=(
            jax.ShapeDtypeStruct((blocks, 2 * width, 2 * states), BF16),
            jax.ShapeDtypeStruct((orbs + blocks, 2 * states), I16),
            jax.ShapeDtypeStruct((blocks, rows, slots * width), I16),
            jax.ShapeDtypeStruct((2 * blocks, slots), F32),
        ),
        in_specs=[far] * 8,
        out_specs=[vm] * 4,
        scratch_shapes=[
            VMEM(wavefunction.shape, F32),
            VMEM(slope_prev.shape, F32),
            VMEM(hopping.shape, BF16),
            VMEM(bond_vectors.shape, F32),
            VMEM(shifts.shape, I32),
            SMEM(counts.shape, I32),
            SMEM(vector_potential.shape, F32),
            DMA((7,)),
        ],
        compiler_params=pltpu.CompilerParams(vmem_limit_bytes=64 * 1024 * 1024),
        name="prep",
    )(wavefunction, slope_prev, hopping, offsets, counts, bond_vectors, shifts, vector_potential)
    size = lax.axis_size("orb")
    up = [(i, (i + 1) % size) for i in range(size)]
    down = [(j, i) for i, j in up]
    before = lax.ppermute(payload, "orb", up)
    after = lax.ppermute(payload, "orb", down)
    tiles = lax.all_gather(part, "st", axis=1, tiled=True)
    return pl.pallas_call(
        slots_kernel,
        out_shape=jax.ShapeDtypeStruct((2, states, orbs), F32),
        in_specs=[vm] * 4 + [far] * 2,
        out_specs=far,
        scratch_shapes=[
            VMEM((3 * blocks, 2 * width, 2 * states), BF16),
            VMEM((2, states, orbs), F32),
            SMEM((2 * blocks, slots), F32),
            SMEM((blocks, slots), I32),
            DMA((2,)),
            DMA((blocks // 2,)),
        ],
        compiler_params=pltpu.CompilerParams(vmem_limit_bytes=40 * 1024 * 1024),
        name="slots",
    )(tiles, own, before, after, phase, offsets)


def solution(mesh):
    return jax.shard_map(
        on_device,
        mesh=mesh,
        in_specs=(
            P(None, "st", "orb"),
            P(None, "st", "orb"),
            P("orb", None, "st", None),
            P("orb", None),
            P("orb"),
            P(None, "orb", None),
            P(None, "orb", None),
            P(),
        ),
        out_specs=P(None, "st", "orb"),
        check_vma=False,
    )
```

```python
import functools

import jax
import jax.numpy as jnp
from jax import lax
from jax.experimental import pallas as pl
from jax.experimental.pallas import tpu as pltpu
from jax.sharding import PartitionSpec as P

VMEM = pltpu.VMEM
SMEM = pltpu.SMEM
DMA = pltpu.SemaphoreType.DMA
F32 = jnp.float32
BF16 = jnp.bfloat16
I16 = jnp.int16
I32 = jnp.int32
LEVELS = 32767.0
STEPS = 256.0
TINY = 1e-37
UP = 71


def split(x):
    hi = x.astype(BF16)
    return hi, (x - hi.astype(F32)).astype(BF16)


def encode(x):
    size = jnp.maximum(jnp.abs(x), TINY)
    down = jnp.floor(-0.0028 - jnp.log2(size))
    digits = jnp.round(x * jnp.exp2(down) * 256.0)
    return (digits * 128.0 + (127.0 - down)).astype(I32).astype(I16)


def decode(code):
    code = jnp.concatenate([x.astype(I32) for x in code], axis=0)
    digits = (code >> 7).astype(F32).astype(BF16)
    return digits * jnp.exp2((code & 127).astype(F32).astype(BF16) - jnp.bfloat16(64))


def tiles_kernel(hop, cnt, bond, shift, vp, part, phase):
    blocks, slots, rows, _ = hop.shape
    for i in range(blocks):
        line = jnp.concatenate([hop[i, s].astype(F32) for s in range(slots)], axis=1)
        part[i] = encode(line)
    theta = jnp.zeros((blocks, slots), F32)
    for k in range(3):
        theta = theta + vp[0:1, k : k + 1] * (bond[k] + 2.0 * shift[k].astype(F32))
    slot = lax.broadcasted_iota(I32, (blocks, blocks), 0)
    live = jnp.where(slot < cnt[...], 2.0**-UP, 0.0).T[:, 0:slots]
    phase[0:blocks] = live * jnp.cos(theta)
    phase[blocks:] = live * jnp.sin(theta)


def segment_kernel(width, wave, slope, own, pay, wave_v, slope_v, sems):
    orbs = wave.shape[2]
    chunk = 256
    copies = []
    for at in range(0, orbs, chunk):
        span = pl.ds(at, chunk)
        for x, x_v in ((wave, wave_v), (slope, slope_v)):
            copies.append(pltpu.make_async_copy(x.at[:, :, span], x_v.at[:, :, span], sems.at[len(copies)]))
            copies[-1].start()
    codes = []
    for c in range(0, orbs, 128):
        if c % chunk == 0:
            for copy in copies[2 * (c // chunk) :][:2]:
                copy.wait()
        cols = pl.ds(c, 128)
        seg = wave_v[:, :, cols] + 0.25 * slope_v[:, :, cols]
        both = jnp.concatenate([seg[0].T, seg[1].T], axis=1)
        hi, lo = split(both)
        for k in range(128 // width):
            j = c // width + k
            span = slice(k * width, (k + 1) * width)
            own[j, 0:width] = hi[span]
            own[j, width : 2 * width] = lo[span]
            top = jnp.maximum(jnp.max(jnp.abs(both[span]), axis=0, keepdims=True), TINY)
            code = jnp.ceil(jnp.log2(top) * STEPS) + 1.0
            codes.append(code)
            q = jnp.round(both[span] * (LEVELS * jnp.exp2(code * (-1.0 / STEPS))))
            pay[j * width : (j + 1) * width] = q.astype(I32).astype(I16)
    pay[orbs:] = jnp.concatenate(codes, axis=0).astype(I32).astype(I16)


def slots_kernel(hop_ref, own_ref, prev_ref, next_ref, phase, off, out, xs, out_v, phase_s, off_s, sems, out_sems):
    peers, blocks, group, depth = hop_ref.shape
    rows = peers * group
    slots = off.shape[1]
    width = depth // slots
    states = out.shape[1]
    phase_copy = pltpu.make_async_copy(phase, phase_s, sems.at[0])
    off_copy = pltpu.make_async_copy(off, off_s, sems.at[1])
    phase_copy.start()
    off_copy.start()

    for j in range(blocks):
        xs[blocks + j] = own_ref[j]
    for base, ref in ((0, prev_ref), (2 * blocks, next_ref)):
        code = ref[blocks * width :].astype(I32).astype(F32)
        scale = jnp.exp2(code * (1.0 / STEPS)) * (1.0 / LEVELS)
        for j in range(blocks):
            q = ref[j * width : (j + 1) * width].astype(I32).astype(F32)
            hi, lo = split(q * scale[j : j + 1])
            xs[base + j, 0:width] = hi
            xs[base + j, width : 2 * width] = lo
    phase_copy.wait()
    off_copy.wait()

    def out_copy(pair):
        cols = pl.ds(pl.multiple_of(pair * 2 * rows, 2 * rows), 2 * rows)
        return pltpu.make_async_copy(out_v.at[:, :, cols], out.at[:, :, cols], out_sems.at[pair])

    def block_pair(pair, _):
        res = []
        for k in range(2):
            i = 2 * pair + k
            a = jnp.zeros((rows, 2 * states), F32)
            b = jnp.zeros((rows, 2 * states), F32)
            for p in range(slots // 2):
                tile = decode([hop_ref[n, i, :, 2 * width * p : 2 * width * (p + 1)] for n in range(peers)])
                for h in range(2):
                    s = 2 * p + h
                    half = tile[:, h * width : (h + 1) * width]
                    prod = jnp.dot(
                        jnp.concatenate([half, half], axis=1),
                        xs[off_s[i, s] + (i + blocks)],
                        preferred_element_type=F32,
                    )
                    a = a + phase_s[i, s] * prod
                    b = b + phase_s[blocks + i, s] * prod
            res.append((a[:, states:] + b[:, :states], b[:, states:] - a[:, :states]))
        cols = pl.ds(pl.multiple_of(pair * 2 * rows, 2 * rows), 2 * rows)
        out_v[0, :, cols] = jnp.concatenate([res[0][0], res[1][0]], axis=0).T
        out_v[1, :, cols] = jnp.concatenate([res[0][1], res[1][1]], axis=0).T
        out_copy(pair).start()
        return 0

    lax.fori_loop(0, blocks // 2, block_pair, 0, unroll=True)
    for pair in range(blocks // 2):
        out_copy(pair).wait()


def on_device(
    wavefunction, slope_prev, hopping, offsets, counts, bond_vectors, shifts, vector_potential
):
    blocks, slots, rows, width = hopping.shape
    states = wavefunction.shape[1]
    orbs = blocks * width
    vm = pl.BlockSpec(memory_space=VMEM)
    far = pl.BlockSpec(memory_space=pltpu.HBM)
    own, payload = pl.pallas_call(
        functools.partial(segment_kernel, width),
        out_shape=(
            jax.ShapeDtypeStruct((blocks, 2 * width, 2 * states), BF16),
            jax.ShapeDtypeStruct((orbs + blocks, 2 * states), I16),
        ),
        in_specs=[far] * 2,
        out_specs=[vm] * 2,
        scratch_shapes=[VMEM(wavefunction.shape, F32), VMEM(slope_prev.shape, F32), DMA((orbs // 128,))],
        compiler_params=pltpu.CompilerParams(vmem_limit_bytes=52 * 1024 * 1024),
        name="segment",
    )(wavefunction, slope_prev)
    part, phase = pl.pallas_call(
        tiles_kernel,
        out_shape=(
            jax.ShapeDtypeStruct((blocks, rows, slots * width), I16),
            jax.ShapeDtypeStruct((2 * blocks, slots), F32),
        ),
        in_specs=[vm] * 5,
        out_specs=[vm] * 2,
        compiler_params=pltpu.CompilerParams(vmem_limit_bytes=40 * 1024 * 1024),
        name="tiles",
    )(hopping, counts[None], bond_vectors, shifts, vector_potential[None])
    size = lax.axis_size("orb")
    up = [(i, (i + 1) % size) for i in range(size)]
    down = [(j, i) for i, j in up]
    before = lax.ppermute(payload, "orb", up)
    after = lax.ppermute(payload, "orb", down)
    tiles = lax.all_gather(part, "st")
    return pl.pallas_call(
        slots_kernel,
        out_shape=jax.ShapeDtypeStruct((2, states, orbs), F32),
        in_specs=[vm] * 4 + [far] * 2,
        out_specs=far,
        scratch_shapes=[
            VMEM((3 * blocks, 2 * width, 2 * states), BF16),
            VMEM((2, states, orbs), F32),
            SMEM((2 * blocks, slots), F32),
            SMEM((blocks, slots), I32),
            DMA((2,)),
            DMA((blocks // 2,)),
        ],
        compiler_params=pltpu.CompilerParams(vmem_limit_bytes=40 * 1024 * 1024),
        name="slots",
    )(tiles, own, before, after, phase, offsets)


def solution(mesh):
    return jax.shard_map(
        on_device,
        mesh=mesh,
        in_specs=(
            P(None, "st", "orb"),
            P(None, "st", "orb"),
            P("orb", None, "st", None),
            P("orb", None),
            P("orb"),
            P(None, "orb", None),
            P(None, "orb", None),
            P(),
        ),
        out_specs=P(None, "st", "orb"),
        check_vma=False,
    )
```

```python
import functools

import jax
import jax.numpy as jnp
from jax import lax
from jax.experimental import pallas as pl
from jax.experimental.pallas import tpu as pltpu
from jax.sharding import PartitionSpec as P

VMEM = pltpu.VMEM
SMEM = pltpu.SMEM
DMA = pltpu.SemaphoreType.DMA
F32 = jnp.float32
BF16 = jnp.bfloat16
I16 = jnp.int16
I32 = jnp.int32
LEVELS = 32767.0
STEPS = 256.0
TINY = 1e-37
UP = 71


def split(x):
    hi = x.astype(BF16)
    return hi, (x - hi.astype(F32)).astype(BF16)


def encode(x):
    size = jnp.maximum(jnp.abs(x), TINY)
    down = jnp.floor(-0.0028 - jnp.log2(size))
    digits = jnp.round(x * jnp.exp2(down) * 256.0)
    return (digits * 128.0 + (127.0 - down)).astype(I32).astype(I16)


def decode(code):
    code = jnp.concatenate([x.astype(I32) for x in code], axis=0)
    digits = (code >> 7).astype(F32).astype(BF16)
    return digits * jnp.exp2((code & 127).astype(F32).astype(BF16) - jnp.bfloat16(64))


def tiles_kernel(hop, cnt, bond, shift, vp, part, phase):
    blocks, slots, rows, _ = hop.shape
    for i in range(blocks):
        line = jnp.concatenate([hop[i, s].astype(F32) for s in range(slots)], axis=1)
        part[i] = encode(line)
    theta = jnp.zeros((blocks, slots), F32)
    for k in range(3):
        theta = theta + vp[0:1, k : k + 1] * (bond[k] + 2.0 * shift[k].astype(F32))
    slot = lax.broadcasted_iota(I32, (blocks, blocks), 0)
    live = jnp.where(slot < cnt[...], 2.0**-UP, 0.0).T[:, 0:slots]
    phase[0:blocks] = live * jnp.cos(theta)
    phase[blocks:] = live * jnp.sin(theta)


def segment_kernel(width, wave, slope, own, pay, wave_v, slope_v, sems):
    orbs = wave.shape[2]
    chunk = 256
    copies = []
    for at in range(0, orbs, chunk):
        span = pl.ds(at, chunk)
        for x, x_v in ((wave, wave_v), (slope, slope_v)):
            copies.append(pltpu.make_async_copy(x.at[:, :, span], x_v.at[:, :, span], sems.at[len(copies)]))
            copies[-1].start()
    codes = []
    for c in range(0, orbs, 128):
        if c % chunk == 0:
            for copy in copies[2 * (c // chunk) :][:2]:
                copy.wait()
        cols = pl.ds(c, 128)
        seg = wave_v[:, :, cols] + 0.25 * slope_v[:, :, cols]
        both = jnp.concatenate([seg[0].T, seg[1].T], axis=1)
        hi, lo = split(both)
        for k in range(128 // width):
            j = c // width + k
            span = slice(k * width, (k + 1) * width)
            own[j, 0:width] = hi[span]
            own[j, width : 2 * width] = lo[span]
            top = jnp.maximum(jnp.max(jnp.abs(both[span]), axis=0, keepdims=True), TINY)
            code = jnp.ceil(jnp.log2(top) * STEPS) + 1.0
            codes.append(code)
            q = jnp.round(both[span] * (LEVELS * jnp.exp2(code * (-1.0 / STEPS))))
            pay[j * width : (j + 1) * width] = q.astype(I32).astype(I16)
    pay[orbs:] = jnp.concatenate(codes, axis=0).astype(I32).astype(I16)


def slots_kernel(hop_ref, own_ref, next_ref, prev_ref, phase, off, out, xs, tiles_v, out_v, phase_s, off_s, sems, out_sems):
    peers, blocks, group, depth = hop_ref.shape
    rows = peers * group
    slots = off.shape[1]
    width = depth // slots
    states = out.shape[1]
    phase_copy = pltpu.make_async_copy(phase, phase_s, sems.at[0])
    off_copy = pltpu.make_async_copy(off, off_s, sems.at[1])
    phase_copy.start()
    off_copy.start()

    for j in range(blocks):
        xs[blocks + j] = own_ref[j]
    for base, ref in ((0, prev_ref), (2 * blocks, next_ref)):
        code = ref[blocks * width :].astype(I32).astype(F32)
        scale = jnp.exp2(code * (1.0 / STEPS)) * (1.0 / LEVELS)
        for j in range(blocks):
            q = ref[j * width : (j + 1) * width].astype(I32).astype(F32)
            hi, lo = split(q * scale[j : j + 1])
            xs[base + j, 0:width] = hi
            xs[base + j, width : 2 * width] = lo
    def left(i, s):
        span = pl.ds(width * (s - s % 2), 2 * width)
        tile = decode([hop_ref[n, i, :, span] for n in range(peers)])
        half = tile[:, s % 2 * width : (s % 2 + 1) * width]
        return jnp.concatenate([half, half], axis=1)

    early = tiles_v.shape[0]
    for i in range(early):
        for s in range(slots):
            tiles_v[i, s] = left(i, s)
    phase_copy.wait()
    off_copy.wait()
    copies = []
    for pair in range(blocks // 2):
        res = []
        for i in (2 * pair, 2 * pair + 1):
            a = jnp.zeros((rows, 2 * states), F32)
            b = jnp.zeros((rows, 2 * states), F32)
            for s in range(slots):
                prod = jnp.dot(
                    tiles_v[i, s] if i < early else left(i, s),
                    xs[off_s[i, s] + (i + blocks)],
                    preferred_element_type=F32,
                )
                a = a + phase_s[i, s] * prod
                b = b + phase_s[blocks + i, s] * prod
            res.append((a[:, states:] + b[:, :states], b[:, states:] - a[:, :states]))
        cols = pl.ds(pair * 2 * rows, 2 * rows)
        out_v[0, :, cols] = jnp.concatenate([res[0][0], res[1][0]], axis=0).T
        out_v[1, :, cols] = jnp.concatenate([res[0][1], res[1][1]], axis=0).T
        copies.append(pltpu.make_async_copy(out_v.at[:, :, cols], out.at[:, :, cols], out_sems.at[pair]))
        copies[-1].start()
    for copy in copies:
        copy.wait()


def on_device(
    wavefunction, slope_prev, hopping, offsets, counts, bond_vectors, shifts, vector_potential
):
    blocks, slots, rows, width = hopping.shape
    states = wavefunction.shape[1]
    orbs = blocks * width
    vm = pl.BlockSpec(memory_space=VMEM)
    far = pl.BlockSpec(memory_space=pltpu.HBM)
    own, payload = pl.pallas_call(
        functools.partial(segment_kernel, width),
        out_shape=(
            jax.ShapeDtypeStruct((blocks, 2 * width, 2 * states), BF16),
            jax.ShapeDtypeStruct((orbs + blocks, 2 * states), I16),
        ),
        in_specs=[far] * 2,
        out_specs=[vm] * 2,
        scratch_shapes=[VMEM(wavefunction.shape, F32), VMEM(slope_prev.shape, F32), DMA((orbs // 128,))],
        compiler_params=pltpu.CompilerParams(vmem_limit_bytes=52 * 1024 * 1024),
        name="segment",
    )(wavefunction, slope_prev)
    part, phase = pl.pallas_call(
        tiles_kernel,
        out_shape=(
            jax.ShapeDtypeStruct((blocks, rows, slots * width), I16),
            jax.ShapeDtypeStruct((2 * blocks, slots), F32),
        ),
        in_specs=[vm] * 5,
        out_specs=[vm] * 2,
        compiler_params=pltpu.CompilerParams(vmem_limit_bytes=40 * 1024 * 1024),
        name="tiles",
    )(hopping, counts[None], bond_vectors, shifts, vector_potential[None])
    size = lax.axis_size("orb")
    up = [(i, (i + 1) % size) for i in range(size)]
    down = [(j, i) for i, j in up]
    before = lax.ppermute(payload, "orb", up)
    after = lax.ppermute(payload, "orb", down)
    tiles = lax.all_gather(part, "st")
    return pl.pallas_call(
        slots_kernel,
        out_shape=jax.ShapeDtypeStruct((2, states, orbs), F32),
        in_specs=[vm] * 4 + [far] * 2,
        out_specs=far,
        scratch_shapes=[
            VMEM((3 * blocks, 2 * width, 2 * states), BF16),
            VMEM((4, slots, rows * lax.axis_size("st"), 2 * width), BF16),
            VMEM((2, states, orbs), F32),
            SMEM((2 * blocks, slots), F32),
            SMEM((blocks, slots), I32),
            DMA((2,)),
            DMA((blocks // 2,)),
        ],
        compiler_params=pltpu.CompilerParams(vmem_limit_bytes=40 * 1024 * 1024),
        name="slots",
    )(tiles, own, after, before, phase, offsets)


def solution(mesh):
    return jax.shard_map(
        on_device,
        mesh=mesh,
        in_specs=(
            P(None, "st", "orb"),
            P(None, "st", "orb"),
            P("orb", None, "st", None),
            P("orb", None),
            P("orb"),
            P(None, "orb", None),
            P(None, "orb", None),
            P(),
        ),
        out_specs=P(None, "st", "orb"),
        check_vma=False,
    )
```

```python
import functools

import jax
import jax.numpy as jnp
from jax import lax
from jax.experimental import pallas as pl
from jax.experimental.pallas import tpu as pltpu
from jax.sharding import PartitionSpec as P

VMEM = pltpu.VMEM
SMEM = pltpu.SMEM
DMA = pltpu.SemaphoreType.DMA
F32 = jnp.float32
BF16 = jnp.bfloat16
I16 = jnp.int16
I32 = jnp.int32
LEVELS = 32767.0
STEPS = 256.0
TINY = 1e-37
UP = 71


def split(x):
    hi = x.astype(BF16)
    return hi, (x - hi.astype(F32)).astype(BF16)


def encode(x):
    size = jnp.maximum(jnp.abs(x), TINY)
    down = jnp.floor(-0.0028 - jnp.log2(size))
    digits = jnp.round(x * jnp.exp2(down) * 256.0)
    return (digits * 128.0 + (127.0 - down)).astype(I32).astype(I16)


def decode(code):
    code = jnp.concatenate([x.astype(I32) for x in code], axis=0)
    digits = (code >> 7).astype(F32).astype(BF16)
    return digits * jnp.exp2((code & 127).astype(F32).astype(BF16) - jnp.bfloat16(64))


def tiles_kernel(hop, cnt, bond, shift, vp, part, phase):
    blocks, slots, rows, _ = hop.shape
    for i in range(blocks):
        line = jnp.concatenate([hop[i, s].astype(F32) for s in range(slots)], axis=1)
        part[i] = encode(line)
    theta = jnp.zeros((blocks, slots), F32)
    for k in range(3):
        theta = theta + vp[0:1, k : k + 1] * (bond[k] + 2.0 * shift[k].astype(F32))
    slot = lax.broadcasted_iota(I32, (blocks, blocks), 0)
    live = jnp.where(slot < cnt[...], 2.0**-UP, 0.0).T[:, 0:slots]
    phase[0:blocks] = live * jnp.cos(theta)
    phase[blocks:] = live * jnp.sin(theta)


def segment_kernel(width, wave, slope, own, pay, wave_v, slope_v, sems):
    orbs = wave.shape[2]
    chunk = 256
    copies = []
    for at in range(0, orbs, chunk):
        span = pl.ds(at, chunk)
        for x, x_v in ((wave, wave_v), (slope, slope_v)):
            copies.append(pltpu.make_async_copy(x.at[:, :, span], x_v.at[:, :, span], sems.at[len(copies)]))
            copies[-1].start()
    codes = []
    for c in range(0, orbs, 128):
        if c % chunk == 0:
            for copy in copies[2 * (c // chunk) :][:2]:
                copy.wait()
        cols = pl.ds(c, 128)
        seg = wave_v[:, :, cols] + 0.25 * slope_v[:, :, cols]
        both = jnp.concatenate([seg[0].T, seg[1].T], axis=1)
        hi, lo = split(both)
        for k in range(128 // width):
            j = c // width + k
            span = slice(k * width, (k + 1) * width)
            own[j, 0:width] = hi[span]
            own[j, width : 2 * width] = lo[span]
            top = jnp.maximum(jnp.max(jnp.abs(both[span]), axis=0, keepdims=True), TINY)
            code = jnp.ceil(jnp.log2(top) * STEPS) + 1.0
            codes.append(code)
            q = jnp.round(both[span] * (LEVELS * jnp.exp2(code * (-1.0 / STEPS))))
            pay[j * width : (j + 1) * width] = q.astype(I32).astype(I16)
    pay[orbs:] = jnp.concatenate(codes, axis=0).astype(I32).astype(I16)


def slots_kernel(hop_ref, own_ref, prev_ref, next_ref, phase, off, out, xs, tiles_v, out_v, phase_s, off_s, sems, out_sems):
    peers, blocks, group, depth = hop_ref.shape
    rows = peers * group
    slots = off.shape[1]
    width = depth // slots
    states = out.shape[1]
    phase_copy = pltpu.make_async_copy(phase, phase_s, sems.at[0])
    off_copy = pltpu.make_async_copy(off, off_s, sems.at[1])
    phase_copy.start()
    off_copy.start()

    for j in range(blocks):
        xs[blocks + j] = own_ref[j]
    for base, ref in ((0, prev_ref), (2 * blocks, next_ref)):
        code = ref[blocks * width :].astype(I32).astype(F32)
        scale = jnp.exp2(code * (1.0 / STEPS)) * (1.0 / LEVELS)
        for j in range(blocks):
            q = ref[j * width : (j + 1) * width].astype(I32).astype(F32)
            hi, lo = split(q * scale[j : j + 1])
            xs[base + j, 0:width] = hi
            xs[base + j, width : 2 * width] = lo
    def left(i, s):
        span = pl.ds(width * (s - s % 2), 2 * width)
        tile = decode([hop_ref[n, i, :, span] for n in range(peers)])
        half = tile[:, s % 2 * width : (s % 2 + 1) * width]
        return jnp.concatenate([half, half], axis=1)

    early = tiles_v.shape[0]
    for i in range(early):
        for s in range(slots):
            tiles_v[i, s] = left(i, s)
    phase_copy.wait()
    off_copy.wait()
    copies = []
    for pair in range(blocks // 2):
        res = []
        for i in (2 * pair, 2 * pair + 1):
            for s in range(slots):
                prod = jnp.dot(
                    tiles_v[i, s] if i < early else left(i, s),
                    xs[off_s[i, s] + (i + blocks)],
                    preferred_element_type=F32,
                )
                cos_term = phase_s[i, s] * prod
                sin_term = phase_s[blocks + i, s] * prod
                a, b = (cos_term, sin_term) if s == 0 else (a + cos_term, b + sin_term)
            res.append((a[:, states:] + b[:, :states], b[:, states:] - a[:, :states]))
        cols = pl.ds(pair * 2 * rows, 2 * rows)
        out_v[0, :, cols] = jnp.concatenate([res[0][0], res[1][0]], axis=0).T
        out_v[1, :, cols] = jnp.concatenate([res[0][1], res[1][1]], axis=0).T
        copies.append(pltpu.make_async_copy(out_v.at[:, :, cols], out.at[:, :, cols], out_sems.at[pair]))
        copies[-1].start()
    for copy in copies:
        copy.wait()


def on_device(
    wavefunction, slope_prev, hopping, offsets, counts, bond_vectors, shifts, vector_potential
):
    blocks, slots, rows, width = hopping.shape
    states = wavefunction.shape[1]
    orbs = blocks * width
    vm = pl.BlockSpec(memory_space=VMEM)
    far = pl.BlockSpec(memory_space=pltpu.HBM)
    own, payload = pl.pallas_call(
        functools.partial(segment_kernel, width),
        out_shape=(
            jax.ShapeDtypeStruct((blocks, 2 * width, 2 * states), BF16),
            jax.ShapeDtypeStruct((orbs + blocks, 2 * states), I16),
        ),
        in_specs=[far] * 2,
        out_specs=[vm] * 2,
        scratch_shapes=[VMEM(wavefunction.shape, F32), VMEM(slope_prev.shape, F32), DMA((orbs // 128,))],
        compiler_params=pltpu.CompilerParams(vmem_limit_bytes=52 * 1024 * 1024),
        name="segment",
    )(wavefunction, slope_prev)
    part, phase = pl.pallas_call(
        tiles_kernel,
        out_shape=(
            jax.ShapeDtypeStruct((blocks, rows, slots * width), I16),
            jax.ShapeDtypeStruct((2 * blocks, slots), F32),
        ),
        in_specs=[vm] * 5,
        out_specs=[vm] * 2,
        compiler_params=pltpu.CompilerParams(vmem_limit_bytes=40 * 1024 * 1024),
        name="tiles",
    )(hopping, counts[None], bond_vectors, shifts, vector_potential[None])
    size = lax.axis_size("orb")
    up = [(i, (i + 1) % size) for i in range(size)]
    down = [(j, i) for i, j in up]
    before = lax.ppermute(payload, "orb", up)
    after = lax.ppermute(payload, "orb", down)
    tiles = lax.all_gather(part, "st")
    return pl.pallas_call(
        slots_kernel,
        out_shape=jax.ShapeDtypeStruct((2, states, orbs), F32),
        in_specs=[vm] * 4 + [far] * 2,
        out_specs=far,
        scratch_shapes=[
            VMEM((3 * blocks, 2 * width, 2 * states), BF16),
            VMEM((4, slots, rows * lax.axis_size("st"), 2 * width), BF16),
            VMEM((2, states, orbs), F32),
            SMEM((2 * blocks, slots), F32),
            SMEM((blocks, slots), I32),
            DMA((2,)),
            DMA((blocks // 2,)),
        ],
        compiler_params=pltpu.CompilerParams(vmem_limit_bytes=40 * 1024 * 1024),
        name="slots",
    )(tiles, own, before, after, phase, offsets)


def solution(mesh):
    return jax.shard_map(
        on_device,
        mesh=mesh,
        in_specs=(
            P(None, "st", "orb"),
            P(None, "st", "orb"),
            P("orb", None, "st", None),
            P("orb", None),
            P("orb"),
            P(None, "orb", None),
            P(None, "orb", None),
            P(),
        ),
        out_specs=P(None, "st", "orb"),
        check_vma=False,
    )
```
